32 devices in a mesh: row: 8 (over y, x, core), col: 4 (over z).
Axes of the slice: x: 2, y: 2, z: 4, core: 2. Of those that a mesh axis runs over, the one named last changes fastest.
Arguments:
- panel_block: bfloat16 [32768, 1024], P(('row', 'col')), may hold values from -1.1953125 to 1.1953125
- block_mask: int32 [256, 8], P(('row', 'col')), may hold values 0 or 1
- grid_pos: int32 [32768], P(('row', 'col')), may hold values from 0 to 32767, as said below
- lower_blocks: bfloat16 [1024, 1024], replicated, may hold values from -0.09375 to 0.09375
- diag_inv: bfloat16 [8, 128, 128], replicated, as said below
- trailing: bfloat16 [32768, 16384], P('row', 'col'), may hold values from -6 to 6
Outputs:
- factor: bfloat16 [32768, 1024], P(('row', 'col'))
- complement: bfloat16 [32768, 16384], P('row', 'col')
The draws below stay inside these ranges and needn't reach their ends.
Inputs may be any that keep to these rules, and one draw needn't show every extreme that they name: grid_pos is a permutation; every aligned block of 1024 entries holds exactly 128 values in each range [r * 4096, (r + 1) * 4096). Each diag_inv[j] is lower triangular.
All inputs are finite; a program needn't handle non-finite values. No bound on the sum of `block_mask` on one device may be relied on, other than what follows from the above.
Results may differ from the reference program's by a relative error of at most 0.0061.
Values may be sent and summed in bfloat16 or wider, within the bound.
A program may use at most 128 MiB of HBM per device.

```python
import jax
import jax.numpy as jnp
from jax import lax

NF = 32768
P_SIZE = 1024
B = 128
ROWS_DEV = 1024
GRID_ROWS = 4096
SLOT = 128
NC = 16384
NB = 256
PB = 8
N_ROW = 8


def draw_grid_pos(key, part):
    row_count = NF // GRID_ROWS
    sources = NF // ROWS_DEV
    key_first, key_second = jax.random.split(key)
    within = jax.vmap(lambda one_key: jax.random.permutation(one_key, GRID_ROWS))(jax.random.split(key_first, row_count))
    absolute = within.astype(jnp.int32) + (jnp.arange(row_count, dtype=jnp.int32) * GRID_ROWS)[:, None]
    by_source = absolute.reshape(row_count, sources, SLOT).transpose(1, 0, 2).reshape(sources, ROWS_DEV)
    shuffled = jax.vmap(lambda one_key: jax.random.permutation(one_key, ROWS_DEV))(jax.random.split(key_second, sources))
    return jnp.take_along_axis(by_source, shuffled.astype(jnp.int32), axis=1).reshape(NF).astype(jnp.int32)


def draw_diag_inv(key, part):
    key_diag, key_off = jax.random.split(key)
    across = jnp.arange(B)
    below = across[:, None] > across[None, :]
    on_diag = across[:, None] == across[None, :]
    diagonal = jax.random.uniform(key_diag, (PB, B, B), jnp.float32, 0.8, 1.2)
    offdiag = jax.random.normal(key_off, (PB, B, B), jnp.float32) * (0.6 / B ** 0.5)
    return jnp.where(on_diag, diagonal, jnp.where(below, offdiag, 0.0)).astype(jnp.bfloat16)


def with_ends(array, stream_key, smallest, largest):
    index_at = [jax.random.randint(jax.random.fold_in(stream_key, axis), (), 0, length) for axis, length in enumerate(array.shape)]
    main_axis = array.shape.index(max(array.shape))
    neighbour = index_at[:main_axis] + [(index_at[main_axis] + 1) % array.shape[main_axis]] + index_at[main_axis + 1:]
    return array.at[tuple(index_at)].set(smallest).at[tuple(neighbour)].set(largest)


def level_of(key, shape, pieces, low, top_value):
    loudness, own = 1.0, jax.random.fold_in(key, 6)
    for dim, blocks in pieces:
        steps = jnp.exp(jax.random.uniform(jax.random.fold_in(own, dim), (blocks,), jnp.float32, low / len(pieces), top_value / len(pieces)))
        loudness = loudness * jnp.repeat(steps, shape[dim] // blocks).reshape([-1 if axis == dim else 1 for axis in range(len(shape))])
    return loudness


def gaussian(rng, extent, deviation, reach, cuts=(), kind=jnp.bfloat16):
    result = jax.random.normal(rng, extent, jnp.float32) * deviation
    if len(cuts) > 0:
        result = level_of(rng, extent, cuts, -0.22, 0.18) * result
    return jnp.clip(result, min=-reach, max=reach).astype(kind)


def setup_inputs(seed: int = 0) -> dict:
    seeds = jax.random.split(jax.random.key(seed), 7)
    return {
        "panel_block": gaussian(seeds[0], (NF, P_SIZE), 0.2, 1.1953125, ((0, 32),)),
        "block_mask": with_ends((jax.random.randint(seeds[1], (NB, PB), 0, 5) < 3).astype(jnp.int32), jax.random.fold_in(seeds[1], 1), 0, 1),
        "grid_pos": draw_grid_pos(jax.random.fold_in(seeds[6], 71), 0),
        "lower_blocks": gaussian(seeds[3], (P_SIZE, P_SIZE), (4 * P_SIZE) ** -0.5, 0.09375),
        "diag_inv": draw_diag_inv(jax.random.fold_in(seeds[6], 71), 0),
        "trailing": gaussian(seeds[5], (NF, NC), 1.0, 6.0, ((0, 8), (1, 4))),
    }


def apply_mask(panel_block, block_mask, block_width):
    row_blocks = panel_block.shape[0] // block_width
    shaped = panel_block.reshape(row_blocks, block_width, block_mask.shape[1], block_width)
    keeping = (block_mask > 0)[:, None, :, None]
    return jnp.where(keeping, shaped, jnp.zeros_like(shaped)).reshape(panel_block.shape)


def solve_panel(masked, lower_blocks, diag_inv):
    block_width = diag_inv.shape[1]
    solved = []
    for block_index in range(diag_inv.shape[0]):
        offset = block_index * block_width
        current = masked[:, offset:offset + block_width].astype(jnp.float32)
        if block_index > 0:
            earlier = jnp.concatenate(solved, axis=1)
            current = current - lax.dot_general(earlier, lower_blocks[offset:offset + block_width, :offset], (((1,), (1,)), ((), ())), preferred_element_type=jnp.float32)
        residue = current.astype(jnp.bfloat16)
        solved.append(lax.dot_general(residue, diag_inv[block_index], (((1,), (1,)), ((), ())), preferred_element_type=jnp.float32).astype(jnp.bfloat16))
    return jnp.concatenate(solved, axis=1)


def reference(panel_block, block_mask, grid_pos, lower_blocks, diag_inv, trailing):
    masked = apply_mask(panel_block, block_mask, B)
    factor = solve_panel(masked, lower_blocks, diag_inv)
    placed = jnp.zeros_like(factor).at[grid_pos].set(factor)
    column_part = placed[:NC]

    def update(inputs):
        trail_tile, left_rows = inputs
        product = lax.dot_general(left_rows, column_part, (((1,), (1,)), ((), ())), preferred_element_type=jnp.float32)
        return (trail_tile.astype(jnp.float32) - product).astype(jnp.bfloat16)

    complement = lax.map(update, (trailing.reshape(N_ROW, GRID_ROWS, NC), placed.reshape(N_ROW, GRID_ROWS, P_SIZE)))
    return factor, complement.reshape(NF, NC)
```

```python
import functools

import jax
import jax.numpy as jnp
from jax import lax
from jax.experimental import pallas as pl
from jax.experimental.pallas import tpu as pltpu
from jax.sharding import PartitionSpec as P

PIECES = 4
EARLY = 3
TRANSPOSED = (((1,), (1,)), ((), ()))


def apply_mask(panel_block, block_mask, block_width):
    row_blocks = panel_block.shape[0] // block_width
    shaped = panel_block.reshape(row_blocks, block_width, block_mask.shape[1], block_width)
    keeping = (block_mask > 0)[:, None, :, None]
    return jnp.where(keeping, shaped, jnp.zeros_like(shaped)).reshape(panel_block.shape)


def solve_block(masked, solved, lower_blocks, diag_inv, block_index):
    block_width = diag_inv.shape[1]
    offset = block_index * block_width
    current = masked[:, offset : offset + block_width].astype(jnp.float32)
    if block_index > 0:
        earlier = jnp.concatenate(solved, axis=1)
        current = current - lax.dot_general(
            earlier,
            lower_blocks[offset : offset + block_width, :offset],
            TRANSPOSED,
            preferred_element_type=jnp.float32,
        )
    residue = current.astype(jnp.bfloat16)
    return lax.dot_general(
        residue, diag_inv[block_index], TRANSPOSED, preferred_element_type=jnp.float32
    ).astype(jnp.bfloat16)


def take_rows(values, order):
    return values.at[order].get(mode="promise_in_bounds", unique_indices=True)


def update_kernel(pieces, *refs):
    left, right = refs[:pieces], refs[pieces : 2 * pieces]
    base_ref, out_ref = refs[2 * pieces], refs[2 * pieces + 1]
    total = None
    for one, other in zip(left, right):
        product = lax.dot_general(
            one[...], other[...], TRANSPOSED, preferred_element_type=jnp.float32
        )
        total = product if total is None else total + product
    out_ref[...] = (base_ref[...].astype(jnp.float32) - total).astype(out_ref.dtype)


def update(left, right, base, in_place):
    pieces = len(left)
    rows, columns = base.shape
    depth = left[0].shape[1]
    tile_m, tile_n = min(512, rows), min(1024, columns)
    spec_left = pl.BlockSpec((tile_m, depth), lambda j, i: (i, 0))
    spec_right = pl.BlockSpec((tile_n, depth), lambda j, i: (j, 0))
    spec_out = pl.BlockSpec((tile_m, tile_n), lambda j, i: (i, j))
    return pl.pallas_call(
        functools.partial(update_kernel, pieces),
        grid=(columns // tile_n, rows // tile_m),
        out_shape=jax.ShapeDtypeStruct(base.shape, base.dtype),
        in_specs=[spec_left] * pieces + [spec_right] * pieces + [spec_out],
        out_specs=spec_out,
        input_output_aliases={2 * pieces: 0} if in_place else {},
        compiler_params=pltpu.CompilerParams(vmem_limit_bytes=40 * 1024 * 1024),
        cost_estimate=pl.CostEstimate(
            flops=2 * rows * columns * depth * pieces,
            bytes_accessed=4 * rows * columns,
            transcendentals=0,
        ),
    )(*left, *right, base)


def local(panel_block, block_mask, grid_pos, lower_blocks, diag_inv, trailing):
    blocks, block_width = diag_inv.shape[0], diag_inv.shape[1]
    rows_dev = panel_block.shape[0]
    grid_rows = trailing.shape[0]
    n_row, n_col = lax.axis_size("row"), lax.axis_size("col")
    slot = rows_dev // n_row
    me_row, me_col = lax.axis_index("row"), lax.axis_index("col")

    sorted_pos, by_grid = lax.sort(
        (grid_pos, lax.iota(jnp.int32, rows_dev)), num_keys=1, is_stable=False
    )
    all_pos = lax.all_gather(sorted_pos, ("row", "col"), axis=0, tiled=False)
    all_pos = all_pos.reshape(n_row, n_col, n_row, slot)
    pos_row = lax.dynamic_index_in_dim(all_pos, me_row, 2, keepdims=False)
    pos_col = lax.dynamic_index_in_dim(all_pos, me_col, 2, keepdims=False)
    keys = jnp.stack([pos_row.transpose(1, 0, 2).reshape(-1), pos_col.reshape(-1)])
    _, orders = lax.sort(
        (keys, lax.broadcasted_iota(jnp.int32, keys.shape, 1)),
        dimension=1,
        num_keys=1,
        is_stable=False,
    )
    order_row, order_col = orders[0], orders[1]

    masked = apply_mask(panel_block, block_mask, block_width)
    solved, row_parts, column_parts = [], [], []
    per_piece = blocks // PIECES
    for piece in range(PIECES):
        for block_index in range(piece * per_piece, (piece + 1) * per_piece):
            solved.append(solve_block(masked, solved, lower_blocks, diag_inv, block_index))
        mine = jnp.concatenate(solved[-per_piece:], axis=1)
        width = mine.shape[1]
        grouped = take_rows(mine, by_grid).reshape(n_row, slot, width)
        arrived = lax.all_to_all(grouped, "row", split_axis=0, concat_axis=0, tiled=True)
        gathered = lax.all_gather(arrived.reshape(-1, width), "col", axis=0, tiled=True)
        row_parts.append(take_rows(gathered, order_row))
        across = lax.all_to_all(grouped[:n_col], "col", split_axis=0, concat_axis=0, tiled=True)
        beside = lax.all_gather(across.reshape(-1, width), "row", axis=0, tiled=True)
        column_parts.append(take_rows(beside, order_col))
    factor = jnp.concatenate(solved, axis=1)
    partial = update(row_parts[:EARLY], column_parts[:EARLY], trailing, False)
    complement = update(row_parts[EARLY:], column_parts[EARLY:], partial, True)
    return (factor, complement)


def solution(mesh):
    placed = (
        P(("row", "col"), None),
        P(("row", "col"), None),
        P(("row", "col")),
        P(),
        P(),
        P("row", "col"),
    )
    return jax.shard_map(
        local,
        mesh=mesh,
        in_specs=placed,
        out_specs=(P(("row", "col"), None), P("row", "col")),
        check_vma=False,
    )
```

```python
import jax
import jax.numpy as jnp
from jax import lax
from jax.sharding import PartitionSpec as P


def apply_mask(panel_block, block_mask, block_width):
    row_blocks = panel_block.shape[0] // block_width
    shaped = panel_block.reshape(row_blocks, block_width, block_mask.shape[1], block_width)
    keeping = (block_mask > 0)[:, None, :, None]
    return jnp.where(keeping, shaped, jnp.zeros_like(shaped)).reshape(panel_block.shape)


def solve_panel(masked, lower_blocks, diag_inv):
    block_width = diag_inv.shape[1]
    solved = []
    for block_index in range(diag_inv.shape[0]):
        offset = block_index * block_width
        current = masked[:, offset : offset + block_width].astype(jnp.float32)
        if block_index > 0:
            earlier = jnp.concatenate(solved, axis=1)
            current = current - lax.dot_general(
                earlier,
                lower_blocks[offset : offset + block_width, :offset],
                (((1,), (1,)), ((), ())),
                preferred_element_type=jnp.float32,
            )
        residue = current.astype(jnp.bfloat16)
        solved.append(
            lax.dot_general(
                residue,
                diag_inv[block_index],
                (((1,), (1,)), ((), ())),
                preferred_element_type=jnp.float32,
            ).astype(jnp.bfloat16)
        )
    return jnp.concatenate(solved, axis=1)


def swap(value, axis, distance):
    count = lax.axis_size(axis)
    return lax.ppermute(value, axis, [(i, i ^ distance) for i in range(count)])


def exchange(groups, axis):
    count, me = lax.axis_size(axis), lax.axis_index(axis)
    parts = []
    for distance in range(count):
        part = lax.dynamic_index_in_dim(groups, me ^ distance, 0, keepdims=False)
        parts.append(swap(part, axis, distance) if distance else part)
    return jnp.concatenate(parts, axis=0)


def spread_row(value):
    count = lax.axis_size("row")
    held = [value] + [swap(value, "row", distance) for distance in range(2, count, 2)]
    held = jnp.concatenate(held, axis=0)
    return jnp.concatenate([held, swap(held, "row", 1)], axis=0)


def gather_col(value):
    count, me = lax.axis_size("col"), lax.axis_index("col")
    held = [value] + [swap(value, "col", distance) for distance in range(1, count)]
    stacked = jnp.stack(held)
    return stacked[me ^ jnp.arange(count)].reshape(-1)


def take_rows(values, order):
    return values.at[order].get(mode="promise_in_bounds", unique_indices=True)


def local(panel_block, block_mask, grid_pos, lower_blocks, diag_inv, trailing):
    block_width = diag_inv.shape[1]
    rows_dev = panel_block.shape[0]
    n_row, n_col = lax.axis_size("row"), lax.axis_size("col")
    slot = rows_dev // n_row
    sorted_pos, by_grid = lax.sort(
        (grid_pos, lax.iota(jnp.int32, rows_dev)), num_keys=1, is_stable=False
    )
    grouped_pos = sorted_pos.reshape(n_row, slot)
    arrived_pos = lax.all_to_all(grouped_pos, "row", split_axis=0, concat_axis=0, tiled=True)
    order_row = jnp.argsort(gather_col(arrived_pos.reshape(-1)))
    order_col = jnp.argsort(spread_row(exchange(grouped_pos[:n_col], "col")))

    masked = apply_mask(panel_block, block_mask, block_width)
    factor = solve_panel(masked, lower_blocks, diag_inv)
    columns = factor.shape[1]
    grouped = take_rows(factor, by_grid).reshape(n_row, slot, columns)
    across = exchange(grouped[:n_col], "col")
    arrived = lax.all_to_all(grouped, "row", split_axis=0, concat_axis=0, tiled=True)
    gathered = lax.all_gather(arrived.reshape(-1, columns), "col", axis=0, tiled=True)
    column_part = take_rows(spread_row(across), order_col)
    row_part = take_rows(gathered, order_row)
    product = lax.dot_general(
        row_part, column_part, (((1,), (1,)), ((), ())), preferred_element_type=jnp.float32
    )
    complement = (trailing.astype(jnp.float32) - product).astype(jnp.bfloat16)
    return (factor, complement)


def solution(mesh):
    placed = (
        P(("row", "col"), None),
        P(("row", "col"), None),
        P(("row", "col")),
        P(),
        P(),
        P("row", "col"),
    )
    return jax.shard_map(
        local,
        mesh=mesh,
        in_specs=placed,
        out_specs=(P(("row", "col"), None), P("row", "col")),
        check_vma=False,
    )
```

```python
import jax
import jax.numpy as jnp
from jax import lax
from jax.sharding import PartitionSpec as P


def apply_mask(panel_block, block_mask, block_width):
    row_blocks = panel_block.shape[0] // block_width
    shaped = panel_block.reshape(row_blocks, block_width, block_mask.shape[1], block_width)
    keeping = (block_mask > 0)[:, None, :, None]
    return jnp.where(keeping, shaped, jnp.zeros_like(shaped)).reshape(panel_block.shape)


def solve_panel(masked, lower_blocks, diag_inv):
    block_width = diag_inv.shape[1]
    solved = []
    for block_index in range(diag_inv.shape[0]):
        offset = block_index * block_width
        current = masked[:, offset : offset + block_width].astype(jnp.float32)
        if block_index > 0:
            earlier = jnp.concatenate(solved, axis=1)
            current = current - lax.dot_general(
                earlier,
                lower_blocks[offset : offset + block_width, :offset],
                (((1,), (1,)), ((), ())),
                preferred_element_type=jnp.float32,
            )
        residue = current.astype(jnp.bfloat16)
        solved.append(
            lax.dot_general(
                residue,
                diag_inv[block_index],
                (((1,), (1,)), ((), ())),
                preferred_element_type=jnp.float32,
            ).astype(jnp.bfloat16)
        )
    return jnp.concatenate(solved, axis=1)


def swap(value, axis, distance):
    count = lax.axis_size(axis)
    return lax.ppermute(value, axis, [(i, i ^ distance) for i in range(count)])


def exchange(groups, axis):
    count, me = lax.axis_size(axis), lax.axis_index(axis)
    parts = []
    for distance in range(count):
        part = lax.dynamic_index_in_dim(groups, me ^ distance, 0, keepdims=False)
        parts.append(swap(part, axis, distance) if distance else part)
    return jnp.concatenate(parts, axis=0)


def spread_row(value):
    count = lax.axis_size("row")
    held = [value] + [swap(value, "row", distance) for distance in range(2, count, 2)]
    held = jnp.concatenate(held, axis=0)
    return jnp.concatenate([held, swap(held, "row", 1)], axis=0)


def gather_col(value):
    count, me = lax.axis_size("col"), lax.axis_index("col")
    held = [value] + [swap(value, "col", distance) for distance in range(1, count)]
    stacked = jnp.stack(held)
    return stacked[me ^ jnp.arange(count)].reshape(-1)


def take_rows(values, order):
    return values.at[order].get(mode="promise_in_bounds", unique_indices=True)


def local(panel_block, block_mask, grid_pos, lower_blocks, diag_inv, trailing):
    block_width = diag_inv.shape[1]
    rows_dev = panel_block.shape[0]
    n_row, n_col = lax.axis_size("row"), lax.axis_size("col")
    slot = rows_dev // n_row
    sorted_pos, by_grid = lax.sort(
        (grid_pos, lax.iota(jnp.int32, rows_dev)), num_keys=1, is_stable=False
    )
    grouped_pos = sorted_pos.reshape(n_row, slot)
    arrived_pos = lax.all_to_all(grouped_pos, "row", split_axis=0, concat_axis=0, tiled=True)
    order_row = jnp.argsort(gather_col(arrived_pos.reshape(-1)))
    order_col = jnp.argsort(spread_row(exchange(grouped_pos[:n_col], "col")))

    masked = apply_mask(panel_block, block_mask, block_width)
    factor = solve_panel(masked, lower_blocks, diag_inv)
    columns = factor.shape[1]
    grouped = take_rows(factor, by_grid).reshape(n_row, slot, columns)
    across = exchange(grouped[:n_col], "col")
    arrived = lax.all_to_all(grouped, "row", split_axis=0, concat_axis=0, tiled=True)
    arrived, across = lax.optimization_barrier((arrived, across))
    gathered = lax.all_gather(arrived.reshape(-1, columns), "col", axis=0, tiled=True)
    column_part = take_rows(spread_row(across), order_col)
    row_part = take_rows(gathered, order_row)
    product = lax.dot_general(
        row_part, column_part, (((1,), (1,)), ((), ())), preferred_element_type=jnp.float32
    )
    complement = (trailing.astype(jnp.float32) - product).astype(jnp.bfloat16)
    return (factor, complement)


def solution(mesh):
    placed = (
        P(("row", "col"), None),
        P(("row", "col"), None),
        P(("row", "col")),
        P(),
        P(),
        P("row", "col"),
    )
    return jax.shard_map(
        local,
        mesh=mesh,
        in_specs=placed,
        out_specs=(P(("row", "col"), None), P("row", "col")),
        check_vma=False,
    )
```
